32 devices in a mesh: ctx: 2 (over core), row: 4 (over y, x), col: 4 (over z).
Axes of the slice: x: 2, y: 2, z: 4, core: 2. Of those that a mesh axis runs over, the one named last changes fastest.
Arguments:
- output_grad: bfloat16 [1024, 8192], P('ctx', ('row', 'col')), may hold values from -6 to 6
- conv_out: bfloat16 [1024, 8192], P('ctx', ('row', 'col')), may hold values from -9 to 9
- input_mix: bfloat16 [1024, 4, 256], P('ctx'), may hold values from -0.5 to 0.5
- output_mix: bfloat16 [1024, 4, 256], P('ctx'), may hold values from -1 to 1
- step_size: float32 [128, 1024], P(('row', 'col'), 'ctx'), may hold values from 0.5 to 2
- log_decay: float32 [128, 1024], P(('row', 'col'), 'ctx'), may hold values from -2.1 to 0, as said below
- skip_gain: float32 [128], P(('row', 'col')), may hold values from 0.5 to 2
- conv_weight: float32 [4, 8192], P(None, ('row', 'col')), may hold values from -3 to 3
- later_grad: float32 [128, 64, 256], P(('row', 'col')), may hold values from -6 to 6
- proj_weight: bfloat16 [8192, 8192], P('col', 'row'), may hold values from -0.0625 to 0.0625
Outputs:
- hidden_grad: bfloat16 [1024, 8192], P('ctx', ('col', 'row'))
- x_grad: bfloat16 [1024, 8192], P('ctx', ('row', 'col'))
- state_grad: float32 [2, 128, 64, 256], P('ctx', ('row', 'col'))
The draws below stay inside these ranges and needn't reach their ends.
Inputs may be any that keep to these rules, and one draw needn't show every extreme that they name: `log_decay`: the forward pass's log decay of each head at each token.
All inputs are finite; a program needn't handle non-finite values.
Results may differ from the reference program's by a relative error of at most 0.022.
Values may be sent and summed in bfloat16 or wider, within the bound.
A program may use at most 128 MiB of HBM per device.

```python
import math
import jax
import jax.numpy as jnp
from jax import lax

D = 8192
HEAD_COUNT = 128
HD = 64
NS = 256
HPG = 32
KW = 4
BLOCK_TOKENS = 512
WINDOW_TOKENS = 1024
P_SIZE = 8192
G = 4
N_CTX = 2


def draw_log_decay(key, part):
    key_rows = jax.random.split(key, 9)
    share = 0.5
    slow_heads = jax.random.uniform(key_rows[0], (HEAD_COUNT, 1)) < share
    quiet_rate = jnp.exp(jax.random.uniform(key_rows[1], (HEAD_COUNT, 1), minval=math.log(0.05), maxval=math.log(0.3))) / BLOCK_TOKENS
    slow_rate = jnp.exp(jax.random.uniform(key_rows[2], (HEAD_COUNT, 1), minval=math.log(0.05), maxval=math.log(0.3))) / WINDOW_TOKENS
    base_rate = jnp.where(slow_heads, slow_rate, quiet_rate)
    stochastic_nudge = jnp.exp(jax.random.uniform(key_rows[3], (HEAD_COUNT, WINDOW_TOKENS), minval=math.log(0.5), maxval=math.log(2.0)))
    factors = jnp.exp(jax.random.uniform(key_rows[4], (N_CTX,), minval=math.log(0.5), maxval=math.log(2.0)))
    segment_scaling_factor = jnp.repeat(factors, BLOCK_TOKENS)
    gentle_portion = -base_rate * stochastic_nudge * segment_scaling_factor[None, :]
    surge_start = jax.random.randint(key_rows[7], (HEAD_COUNT, N_CTX), BLOCK_TOKENS // 2, BLOCK_TOKENS - 7)
    starting_points = jnp.repeat(surge_start, BLOCK_TOKENS, axis=1)
    offset_within_block = jnp.arange(WINDOW_TOKENS) % BLOCK_TOKENS
    inside_surge = (offset_within_block[None, :] >= starting_points) & (offset_within_block[None, :] < starting_points + 8)
    surge_depth = jnp.exp(jax.random.uniform(key_rows[8], (HEAD_COUNT, WINDOW_TOKENS), minval=math.log(0.75), maxval=math.log(1.5)))
    rapid_portion = jnp.where(inside_surge, -surge_depth, gentle_portion)
    head_values = jnp.where(slow_heads, gentle_portion, rapid_portion)
    marked_locations = jax.random.randint(key_rows[5], (3,), 0, WINDOW_TOKENS)
    objective_numbers = jax.random.uniform(key_rows[6], (3,), minval=0.2, maxval=0.4)
    token_places = jnp.arange(WINDOW_TOKENS)
    spike_occurrences = jnp.sum(jnp.where(token_places[None, :] == marked_locations[:, None], jnp.log(1.0 - objective_numbers)[:, None], 0.0), axis=0)
    return (head_values + spike_occurrences[None, :]).astype(jnp.float32)


def block_levels(own_key, dims, cuts, least, largest):
    factor_of = 1.0
    for axis_at, blocks in cuts:
        steps = jax.random.uniform(jax.random.fold_in(jax.random.fold_in(own_key, 6), axis_at), (blocks,), jnp.float32, least / len(cuts), largest / len(cuts))
        factor_of = factor_of * jnp.repeat(jnp.exp(steps), dims[axis_at] // blocks).reshape((-1,) + (1,) * (len(dims) - 1 - axis_at))
    return factor_of


def bell_draw(rng, shape, deviation, reach, cuts=(), kind=jnp.bfloat16):
    drawn = jax.random.normal(rng, shape, jnp.float32) * deviation
    if len(cuts) > 0:
        drawn = block_levels(rng, shape, cuts, -0.22, 0.18) * drawn
    return jnp.clip(drawn, min=-reach, max=reach).astype(kind)


def setup_inputs(seed: int = 0) -> dict:
    key_of = jax.random.split(jax.random.key(seed), 11)
    return {
        "output_grad": bell_draw(key_of[0], (WINDOW_TOKENS, P_SIZE), 1.0, 6.0, ((0, 2), (1, 16))),
        "conv_out": bell_draw(key_of[1], (WINDOW_TOKENS, P_SIZE), 1.5, 9.0, ((0, 2), (1, 16))),
        "input_mix": bell_draw(key_of[2], (WINDOW_TOKENS, G, NS), (WINDOW_TOKENS ** -0.5), 0.5, ((0, 2),)),
        "output_mix": bell_draw(key_of[3], (WINDOW_TOKENS, G, NS), (NS ** -0.5), 1.0, ((0, 2),)),
        "step_size": jnp.clip(jnp.exp(math.log(2.0) - 1.3862944 * jax.random.uniform(key_of[4], (HEAD_COUNT, WINDOW_TOKENS), jnp.float32) ** block_levels(key_of[4], (HEAD_COUNT, WINDOW_TOKENS), ((0, 16), (1, 2)), -0.2, 0.2)), 0.5, 2.0),
        "log_decay": draw_log_decay(jax.random.fold_in(key_of[10], 71), 0),
        "skip_gain": jnp.clip(jnp.exp(math.log(2.0) - 1.3862944 * jax.random.uniform(key_of[6], (HEAD_COUNT,), jnp.float32) ** block_levels(key_of[6], (HEAD_COUNT,), ((0, 16),), -0.2, 0.2)), 0.5, 2.0),
        "conv_weight": bell_draw(key_of[7], (KW, P_SIZE), 0.5, 3.0, ((1, 16),), jnp.float32),
        "later_grad": bell_draw(key_of[8], (HEAD_COUNT, HD, NS), ((WINDOW_TOKENS / NS) ** 0.5), 6.0, ((0, 16),), jnp.float32),
        "proj_weight": bell_draw(key_of[9], (D, P_SIZE), P_SIZE ** -0.5, 0.0625, ((0, 4), (1, 4))),
    }


def reference(output_grad, conv_out, input_mix, output_mix, step_size, log_decay, skip_gain, conv_weight, later_grad, proj_weight):
    per_head = output_grad.reshape(WINDOW_TOKENS, HEAD_COUNT, HD)
    group_of = jnp.arange(HEAD_COUNT) // HPG
    positions = jnp.arange(BLOCK_TOKENS)
    causal = positions[None, :] >= positions[:, None]

    def one_block(carried, block_index):
        start = (block_index * BLOCK_TOKENS).astype(jnp.int32)
        grads = lax.dynamic_slice_in_dim(per_head, start, BLOCK_TOKENS, 0).astype(jnp.float32)
        write_rows = lax.dynamic_slice_in_dim(input_mix, start, BLOCK_TOKENS, 0).astype(jnp.float32)
        read_rows = lax.dynamic_slice_in_dim(output_mix, start, BLOCK_TOKENS, 0).astype(jnp.float32)
        decay_rows = lax.dynamic_slice_in_dim(log_decay, start, BLOCK_TOKENS, 1)
        steps_here = lax.dynamic_slice_in_dim(step_size, start, BLOCK_TOKENS, 1)
        cumulative = jnp.cumsum(decay_rows, axis=1)
        block_end = cumulative[:, -1]
        scores = jnp.einsum("tgn,sgn->gts", write_rows, read_rows)
        head_scores = scores[group_of]
        offsets = cumulative[:, None, :] - cumulative[:, :, None]
        mixing = (jnp.exp(jnp.where(causal[None], offsets, -jnp.inf)) * head_scores).astype(jnp.bfloat16)
        intra = jnp.einsum("hts,shd->thd", mixing.astype(jnp.float32), grads)
        weighted = (jnp.exp(cumulative).T[:, :, None] * grads).astype(jnp.bfloat16)
        head_reads = read_rows[:, group_of, :]
        head_writes = write_rows[:, group_of, :]
        block_sum = jnp.einsum("shd,shn->hdn", weighted.astype(jnp.float32), head_reads)
        inter = jnp.einsum("hdn,thn->thd", carried, head_writes, precision=lax.Precision.HIGHEST)
        inter = inter * jnp.exp(block_end[:, None] - cumulative).T[:, :, None]
        input_grad = steps_here.T[:, :, None] * (intra + inter) + skip_gain[None, :, None] * grads
        state_start = block_sum + jnp.exp(block_end)[:, None, None] * carried
        return state_start, (input_grad, state_start)

    order = jnp.arange(N_CTX - 1, -1, -1).astype(jnp.int32)
    unused, stacked = lax.scan(one_block, later_grad, order)
    input_grads = jnp.flip(stacked[0], axis=0).reshape(WINDOW_TOKENS, P_SIZE)
    state_grad = jnp.flip(stacked[1], axis=0)
    activated = conv_out.astype(jnp.float32)
    sigma = jax.nn.sigmoid(activated)
    pre_grad = (input_grads * sigma * (1.0 + activated * (1.0 - sigma))).astype(jnp.bfloat16)
    extended = jnp.concatenate([pre_grad.astype(jnp.float32), jnp.zeros((KW - 1, P_SIZE), jnp.float32)], axis=0)
    accum = jnp.zeros((WINDOW_TOKENS, P_SIZE), jnp.float32)
    for tap in range(KW):
        accum = accum + conv_weight[tap][None, :] * extended[tap:tap + WINDOW_TOKENS]
    x_grad = accum.astype(jnp.bfloat16)
    hidden_grad = jnp.dot(x_grad, proj_weight.T, preferred_element_type=jnp.float32).astype(jnp.bfloat16)
    return hidden_grad, x_grad, state_grad
```

```python
import functools

import jax
import jax.numpy as jnp
from jax import lax
from jax.experimental import pallas as pl
from jax.experimental.pallas import tpu as pltpu
from jax.sharding import PartitionSpec as P

HD = 64
HPG = 32
KW = 4
CHUNKS = 4
REACH = 2


def from_behind(value, axis, steps):
    count = lax.axis_size(axis)
    first, last = (max(0, -steps), min(count, count - steps))
    return lax.ppermute(value, axis, [(source, source + steps) for source in range(first, last)])


def project_kernel(
    n_row,
    n_col,
    x_ref,
    w_hbm,
    out_ref,
    w_ref,
    gathered,
    staged,
    landed,
    own,
    w_sem,
    col_send,
    col_recv,
    fwd_send,
    row_send,
    row_recv,
):
    row = lax.axis_index("row")
    col = lax.axis_index("col")
    step = gathered.shape[2]
    width = gathered.shape[3]
    d_out = out_ref.shape[1]
    mesh_id = pl.DeviceIdType.MESH

    load_w = pltpu.make_async_copy(w_hbm, w_ref, w_sem)
    load_w.start()

    barrier = pltpu.get_barrier_semaphore()
    for j in range(1, n_row):
        pl.semaphore_signal(
            barrier, inc=1, device_id={"row": lax.rem(row + j, n_row)}, device_id_type=mesh_id
        )
    for j in range(1, n_col):
        pl.semaphore_signal(
            barrier, inc=1, device_id={"col": lax.rem(col + j, n_col)}, device_id_type=mesh_id
        )
    pl.semaphore_wait(barrier, n_row + n_col - 2)

    deltas = [d for d in range(-REACH, REACH + 1) if d != 0]

    def col_copy(chunk, owner, target, sem):
        return pltpu.make_async_remote_copy(
            src_ref=gathered.at[chunk, owner],
            dst_ref=gathered.at[chunk, owner],
            send_sem=sem,
            recv_sem=col_recv.at[chunk, owner],
            device_id={"col": target},
            device_id_type=mesh_id,
        )

    def each_send(chunk, act):
        for at, delta in enumerate(deltas):
            target = col + delta

            @pl.when((target >= 0) & (target < n_col))
            def _():
                act(col_copy(chunk, col, target, col_send.at[chunk, at]))

    def send_chunk(chunk):
        gathered[chunk, col] = x_ref[pl.ds(pl.multiple_of(chunk * step, step), step), :]
        each_send(chunk, lambda copy: copy.start())

    def each_arrival(chunk, receive, forward):
        for side, sign in enumerate((-1, 1)):
            for dist in list(range(REACH, n_col)) + list(range(1, REACH)):
                owner = col + sign * dist

                @pl.when((owner >= 0) & (owner < n_col))
                def _():
                    if receive:
                        col_copy(chunk, owner, col, fwd_send.at[chunk, side, dist]).wait_recv()
                    if dist >= REACH:
                        target = col - sign

                        @pl.when((target >= 0) & (target < n_col))
                        def _():
                            forward(
                                col_copy(chunk, owner, target, fwd_send.at[chunk, side, dist])
                            )

    def row_copy(chunk, target):
        return pltpu.make_async_remote_copy(
            src_ref=staged.at[chunk, target],
            dst_ref=landed.at[chunk, row],
            send_sem=row_send.at[chunk, target],
            recv_sem=row_recv.at[chunk, row],
            device_id={"row": target},
            device_id_type=mesh_id,
        )

    def finish(chunk):
        total = own[chunk]
        for j in range(1, n_row):
            source = lax.rem(row + j, n_row)
            pltpu.make_async_remote_copy(
                src_ref=staged.at[chunk, source],
                dst_ref=landed.at[chunk, source],
                send_sem=row_send.at[chunk, source],
                recv_sem=row_recv.at[chunk, source],
                device_id={"row": source},
                device_id_type=mesh_id,
            ).wait_recv()
            total = total + landed[chunk, source].astype(jnp.float32)
        out_ref[pl.ds(pl.multiple_of(chunk * step, step), step), :] = total.astype(out_ref.dtype)

    def product(chunk, target):
        rows = pl.ds(pl.multiple_of(target * d_out, d_out), d_out)
        total = None
        for owner in range(n_col):
            part = lax.dot_general(
                gathered[chunk, owner],
                w_ref[rows, owner * width : (owner + 1) * width],
                (((1,), (1,)), ((), ())),
                preferred_element_type=jnp.float32,
            )
            total = part if total is None else total + part
        return total

    send_chunk(0)
    send_chunk(1)
    load_w.wait()

    def turn(chunk, carry):
        each_arrival(chunk, True, lambda copy: copy.start())
        each_send(chunk, lambda copy: copy.wait_send())

        @pl.when(chunk + 2 < CHUNKS)
        def _():
            send_chunk(chunk + 2)

        @pl.loop(1, n_row)
        def _(j):
            target = lax.rem(row + j, n_row)
            staged[chunk, target] = product(chunk, target).astype(jnp.bfloat16)
            row_copy(chunk, target).start()

        own[chunk] = product(chunk, row)

        @pl.when(chunk > 0)
        def _():
            finish(chunk - 1)

        return carry

    lax.fori_loop(0, CHUNKS, turn, 0)
    finish(CHUNKS - 1)

    def drain(chunk, carry):
        each_arrival(chunk, False, lambda copy: copy.wait_send())
        for j in range(1, n_row):
            row_copy(chunk, lax.rem(row + j, n_row)).wait_send()
        return carry

    lax.fori_loop(0, CHUNKS, drain, 0)


def project(x_grad, proj_weight):
    n_row, n_col = lax.axis_size("row"), lax.axis_size("col")
    tokens, width = x_grad.shape
    step = tokens // CHUNKS
    d_out = proj_weight.shape[0] // n_row
    return pl.pallas_call(
        functools.partial(project_kernel, n_row, n_col),
        out_shape=jax.ShapeDtypeStruct((tokens, d_out), jnp.bfloat16),
        in_specs=[
            pl.BlockSpec(memory_space=pltpu.VMEM),
            pl.BlockSpec(memory_space=pl.ANY),
        ],
        out_specs=pl.BlockSpec(memory_space=pltpu.VMEM),
        scratch_shapes=[
            pltpu.VMEM(proj_weight.shape, jnp.bfloat16),
            pltpu.VMEM((CHUNKS, n_col, step, width), jnp.bfloat16),
            pltpu.VMEM((CHUNKS, n_row, step, d_out), jnp.bfloat16),
            pltpu.VMEM((CHUNKS, n_row, step, d_out), jnp.bfloat16),
            pltpu.VMEM((CHUNKS, step, d_out), jnp.float32),
            pltpu.SemaphoreType.DMA,
            pltpu.SemaphoreType.DMA((CHUNKS, 2 * REACH)),
            pltpu.SemaphoreType.DMA((CHUNKS, n_col)),
            pltpu.SemaphoreType.DMA((CHUNKS, 2, n_col)),
            pltpu.SemaphoreType.DMA((CHUNKS, n_row)),
            pltpu.SemaphoreType.DMA((CHUNKS, n_row)),
        ],
        compiler_params=pltpu.CompilerParams(
            collective_id=0, has_side_effects=True, vmem_limit_bytes=48 << 20
        ),
        cost_estimate=pl.CostEstimate(
            flops=2 * tokens * proj_weight.shape[0] * proj_weight.shape[1],
            bytes_accessed=2 * proj_weight.shape[0] * proj_weight.shape[1],
            transcendentals=0,
        ),
    )(x_grad, proj_weight)


def on_device(
    output_grad,
    conv_out,
    input_mix,
    output_mix,
    step_size,
    log_decay,
    skip_gain,
    conv_weight,
    later_grad,
    proj_weight,
):
    tokens_dev = output_grad.shape[0]
    heads_dev = step_size.shape[0]
    head_block = lax.axis_index("row") * lax.axis_size("col") + lax.axis_index("col")
    group = head_block * heads_dev // HPG
    write_rows = lax.dynamic_index_in_dim(input_mix, group, 1, keepdims=False)
    read_rows = lax.dynamic_index_in_dim(output_mix, group, 1, keepdims=False)
    cumulative = jnp.cumsum(log_decay, axis=1)
    block_end = cumulative[:, -1]
    decays = jnp.exp(block_end)
    per_head = output_grad.reshape(tokens_dev, heads_dev, HD)
    weighted = (jnp.exp(cumulative).T[:, :, None] * per_head.astype(jnp.float32)).astype(
        jnp.bfloat16
    )
    block_sum = jnp.einsum("shd,sn->hdn", weighted, read_rows, preferred_element_type=jnp.float32)
    is_last = lax.axis_index("ctx") == lax.axis_size("ctx") - 1

    def chain_turn(turn_index, estimate):
        passed = from_behind(
            (block_sum + decays[:, None, None] * estimate).astype(jnp.bfloat16), "ctx", -1
        ).astype(jnp.float32)
        return jnp.where(is_last, later_grad, passed)

    carried = lax.fori_loop(
        0,
        lax.axis_size("ctx") - 1,
        chain_turn,
        jnp.where(is_last, later_grad, jnp.zeros_like(later_grad)),
    )
    state_start = block_sum + decays[:, None, None] * carried
    scores = jnp.dot(write_rows, read_rows.T, preferred_element_type=jnp.float32)
    positions = jnp.arange(tokens_dev)
    causal = positions[None, :] >= positions[:, None]
    offsets = cumulative[:, None, :] - cumulative[:, :, None]
    mixing = (jnp.exp(jnp.where(causal[None], offsets, -jnp.inf)) * scores[None]).astype(
        jnp.bfloat16
    )
    intra = jnp.einsum("hts,shd->thd", mixing, per_head, preferred_element_type=jnp.float32)
    inter = jnp.einsum(
        "hdn,tn->thd", carried, write_rows.astype(jnp.float32), precision=lax.Precision.HIGHEST
    )
    inter = inter * jnp.exp(block_end[:, None] - cumulative).T[:, :, None]
    input_grad = step_size.T[:, :, None] * (intra + inter) + skip_gain[
        None, :, None
    ] * per_head.astype(jnp.float32)
    flat_grad = input_grad.reshape(tokens_dev, heads_dev * HD)
    activated = conv_out.astype(jnp.float32)
    sigma = jax.nn.sigmoid(activated)
    pre_grad = (flat_grad * sigma * (1.0 + activated * (1.0 - sigma))).astype(jnp.bfloat16)
    rim_rows = from_behind(pre_grad[: KW - 1], "ctx", -1)
    extended = jnp.concatenate([pre_grad, rim_rows], axis=0).astype(jnp.float32)
    accum = jnp.zeros(pre_grad.shape, jnp.float32)
    for tap in range(KW):
        accum = accum + conv_weight[tap][None, :] * extended[tap : tap + tokens_dev]
    x_grad = accum.astype(jnp.bfloat16)
    hidden_grad = project(x_grad, proj_weight)
    return (hidden_grad, x_grad, state_start[None])


def solution(mesh):
    return jax.shard_map(
        on_device,
        mesh=mesh,
        in_specs=(
            P("ctx", ("row", "col")),
            P("ctx", ("row", "col")),
            P("ctx", None, None),
            P("ctx", None, None),
            P(("row", "col"), "ctx"),
            P(("row", "col"), "ctx"),
            P(("row", "col")),
            P(None, ("row", "col")),
            P(("row", "col"), None, None),
            P("col", "row"),
        ),
        out_specs=(
            P("ctx", ("col", "row")),
            P("ctx", ("row", "col")),
            P("ctx", ("row", "col"), None, None),
        ),
        check_vma=False,
    )
```

```python
import functools

import jax
import jax.numpy as jnp
from jax import lax
from jax.experimental import pallas as pl
from jax.experimental.pallas import tpu as pltpu
from jax.sharding import PartitionSpec as P

HD = 64
HPG = 32
KW = 4
CHUNKS = 4
REACH = 2
FLYING = 2
RIM = 16


def layer_kernel(
    n_ctx,
    n_row,
    n_col,
    grad_ref,
    conv_ref,
    write_ref,
    read_ref,
    step_ref,
    decay_ref,
    skip_ref,
    tap_ref,
    later_ref,
    w_hbm,
    out_ref,
    x_ref,
    state_ref,
    w_ref,
    pre_ref,
    carried_ref,
    state_out,
    state_in,
    rim_out,
    rim_in,
    gathered,
    staged,
    landed,
    own,
    w_sem,
    col_send,
    col_recv,
    fwd_send,
    row_send,
    row_recv,
    ctx_send,
    ctx_recv,
):
    ctx = lax.axis_index("ctx")
    row = lax.axis_index("row")
    col = lax.axis_index("col")
    step = gathered.shape[2]
    width = gathered.shape[3]
    d_out = out_ref.shape[1]
    mesh_id = pl.DeviceIdType.MESH

    load_w = pltpu.make_async_copy(w_hbm, w_ref, w_sem)
    load_w.start()

    barrier = pltpu.get_barrier_semaphore()
    for j in range(1, n_row):
        pl.semaphore_signal(
            barrier, inc=1, device_id={"row": lax.rem(row + j, n_row)}, device_id_type=mesh_id
        )
    for j in range(1, n_col):
        pl.semaphore_signal(
            barrier, inc=1, device_id={"col": lax.rem(col + j, n_col)}, device_id_type=mesh_id
        )
    has_next, has_previous = ctx < n_ctx - 1, ctx > 0
    for there, delta in ((has_next, 1), (has_previous, -1)):

        @pl.when(there)
        def _():
            pl.semaphore_signal(
                barrier, inc=1, device_id={"ctx": ctx + delta}, device_id_type=mesh_id
            )

    deltas = [d for d in range(-REACH, REACH + 1) if d != 0]

    def col_copy(chunk, owner, target, sem):
        return pltpu.make_async_remote_copy(
            src_ref=gathered.at[chunk, owner],
            dst_ref=gathered.at[chunk, owner],
            send_sem=sem,
            recv_sem=col_recv.at[chunk, owner],
            device_id={"col": target},
            device_id_type=mesh_id,
        )

    def each_send(chunk, act):
        for at, delta in enumerate(deltas):
            target = col + delta

            @pl.when((target >= 0) & (target < n_col))
            def _():
                act(col_copy(chunk, col, target, col_send.at[chunk, at]))

    def send_chunk(chunk):
        each_send(chunk, lambda copy: copy.start())

    def each_arrival(chunk, receive, forward):
        for side, sign in enumerate((-1, 1)):
            for dist in list(range(REACH, n_col)) + list(range(1, REACH)):
                owner = col + sign * dist

                @pl.when((owner >= 0) & (owner < n_col))
                def _():
                    if receive:
                        col_copy(chunk, owner, col, fwd_send.at[chunk, side, dist]).wait_recv()
                    if dist >= REACH:
                        target = col - sign

                        @pl.when((target >= 0) & (target < n_col))
                        def _():
                            forward(
                                col_copy(chunk, owner, target, fwd_send.at[chunk, side, dist])
                            )

    def row_copy(chunk, target):
        return pltpu.make_async_remote_copy(
            src_ref=staged.at[chunk, target],
            dst_ref=landed.at[chunk, row],
            send_sem=row_send.at[chunk, target],
            recv_sem=row_recv.at[chunk, row],
            device_id={"row": target},
            device_id_type=mesh_id,
        )

    def finish(chunk):
        total = own[chunk]
        for j in range(1, n_row):
            source = lax.rem(row + j, n_row)
            pltpu.make_async_remote_copy(
                src_ref=staged.at[chunk, source],
                dst_ref=landed.at[chunk, source],
                send_sem=row_send.at[chunk, source],
                recv_sem=row_recv.at[chunk, source],
                device_id={"row": source},
                device_id_type=mesh_id,
            ).wait_recv()
            total = total + landed[chunk, source].astype(jnp.float32)
        first = pl.multiple_of((CHUNKS - 1 - chunk) * step, step)
        out_ref[pl.ds(first, step), :] = total.astype(out_ref.dtype)

    def product(chunk, target):
        rows = pl.ds(pl.multiple_of(target * d_out, d_out), d_out)
        total = None
        for owner in range(n_col):
            part = lax.dot_general(
                gathered[chunk, owner],
                w_ref[rows, owner * width : (owner + 1) * width],
                (((1,), (1,)), ((), ())),
                preferred_element_type=jnp.float32,
            )
            total = part if total is None else total + part
        return total

    def ctx_copy(at, source, target):
        return pltpu.make_async_remote_copy(
            src_ref=source,
            dst_ref=target,
            send_sem=ctx_send.at[at],
            recv_sem=ctx_recv.at[at],
            device_id={"ctx": lax.rem(ctx + n_ctx - 1, n_ctx)},
            device_id_type=mesh_id,
        )

    pass_state = ctx_copy(0, state_out, state_in)
    pass_rim = ctx_copy(1, rim_out, rim_in)

    tokens = grad_ref.shape[0]
    heads = decay_ref.shape[0]
    pairs = heads // 2
    lanes = 2 * HD
    f32, bf16 = jnp.float32, jnp.bfloat16

    def dot(a, b, a_dim, b_dim):
        return lax.dot_general(
            a, b, (((a_dim,), (b_dim,)), ((), ())), preferred_element_type=f32
        )

    decay = decay_ref[...]
    high = decay.astype(bf16)
    rest = decay - high.astype(f32)
    middle = rest.astype(bf16)
    low = (rest - middle.astype(f32)).astype(bf16)
    upto = lax.broadcasted_iota(jnp.int32, (tokens, tokens), 0) <= lax.broadcasted_iota(
        jnp.int32, (tokens, tokens), 1
    )
    triangle = upto.astype(f32).astype(bf16)
    cumulative = (
        dot(high, triangle, 1, 0) + dot(middle, triangle, 1, 0) + dot(low, triangle, 1, 0)
    )
    by_token = cumulative.T
    steps = step_ref[...].T
    grown = jnp.exp(by_token)
    left = jnp.exp(by_token[tokens - 1 : tokens, :] - by_token)

    def spread(columns, pair, count):
        lane = lax.broadcasted_iota(jnp.int32, (count, lanes), 1)
        return jnp.where(
            lane < HD, columns[:, 2 * pair : 2 * pair + 1], columns[:, 2 * pair + 1 : 2 * pair + 2]
        )

    weighted = jnp.concatenate(
        [
            (
                spread(grown, pair, tokens)
                * grad_ref[:, pair * lanes : (pair + 1) * lanes].astype(f32)
            ).astype(bf16)
            for pair in range(pairs)
        ],
        axis=1,
    )
    block_sum = dot(weighted, read_ref[...], 0, 0)

    total_signals = n_row + n_col - 2 + has_next.astype(jnp.int32) + has_previous.astype(jnp.int32)
    pl.semaphore_wait(barrier, total_signals)

    @pl.when(has_next)
    def _():
        pass_state.wait_recv()
        carried_ref[...] = state_in[...].astype(f32)

    @pl.when(jnp.logical_not(has_next))
    def _():
        carried_ref[...] = later_ref[...]

    for head in range(heads):
        rows = slice(head * HD, (head + 1) * HD)
        factor = jnp.exp(cumulative[head : head + 1, tokens - 1 : tokens])
        state = block_sum[rows] + factor * carried_ref[rows, :]
        state_ref[rows, :] = state
        state_out[rows, :] = state.astype(bf16)

    @pl.when(has_previous)
    def _():
        pass_state.start()

    carried = carried_ref[...].astype(bf16)

    def pre_rows(start, count):
        rows = slice(start, start + count)
        span = tokens - start
        write = write_ref[rows, :]
        scores = dot(write, read_ref[start:, :], 1, 1)
        later = lax.broadcasted_iota(jnp.int32, (count, span), 1) >= lax.broadcasted_iota(
            jnp.int32, (count, span), 0
        )
        scores = jnp.where(later, scores, 0.0)
        inter = dot(write, carried, 1, 1)
        lane = lax.broadcasted_iota(jnp.int32, (count, lanes), 1)
        found = []
        for pair in range(pairs):
            columns = slice(pair * lanes, (pair + 1) * lanes)
            mixing = []
            for head in (2 * pair, 2 * pair + 1):
                offset = cumulative[head : head + 1, start:] - by_token[rows, head : head + 1]
                mixing.append((jnp.exp(jnp.minimum(offset, 0.0)) * scores).astype(bf16))
            both = dot(jnp.concatenate(mixing, axis=0), grad_ref[start:, columns], 1, 0)
            intra = jnp.where(lane < HD, both[:count], both[count:])
            summed = intra + inter[:, columns] * spread(left[rows], pair, count)
            value = (
                spread(steps[rows], pair, count) * summed
                + skip_ref[:, columns] * grad_ref[rows, columns].astype(f32)
            )
            v = conv_ref[rows, columns].astype(f32)
            q = 1.0 / (1.0 + jnp.exp(-v))
            found.append((value * q * (1.0 + v * (1.0 - q))).astype(bf16))
        return jnp.concatenate(found, axis=1)

    @pl.when(has_previous)
    def _():
        rim_out[...] = pre_rows(0, RIM)
        pass_rim.start()

    for chunk in range(CHUNKS):
        start = tokens - (chunk + 1) * step
        pre_ref[start : start + step, :] = pre_rows(start, step).astype(f32)
        if chunk == 0:

            @pl.when(has_next)
            def _():
                pass_rim.wait_recv()
                pre_ref[tokens:, :] = rim_in[...].astype(f32)

            @pl.when(jnp.logical_not(has_next))
            def _():
                pre_ref[tokens:, :] = jnp.zeros((RIM, pre_ref.shape[1]), f32)

        mixed = tap_ref[0:1, :] * pre_ref[start : start + step, :]
        for tap in range(1, KW):
            mixed = mixed + tap_ref[tap : tap + 1, :] * pre_ref[start + tap : start + tap + step, :]
        mixed = mixed.astype(bf16)
        x_ref[start : start + step, :] = mixed
        gathered[chunk, col] = mixed
        if chunk < FLYING:
            send_chunk(chunk)
    load_w.wait()

    def turn(chunk, carry):
        each_arrival(chunk, True, lambda copy: copy.start())
        each_send(chunk, lambda copy: copy.wait_send())

        @pl.when(chunk + FLYING < CHUNKS)
        def _():
            send_chunk(chunk + FLYING)

        @pl.loop(1, n_row)
        def _(j):
            target = lax.rem(row + j, n_row)
            staged[chunk, target] = product(chunk, target).astype(jnp.bfloat16)
            row_copy(chunk, target).start()

        own[chunk] = product(chunk, row)

        @pl.when(chunk > 0)
        def _():
            finish(chunk - 1)

        return carry

    lax.fori_loop(0, CHUNKS, turn, 0)
    finish(CHUNKS - 1)

    def drain(chunk, carry):
        each_arrival(chunk, False, lambda copy: copy.wait_send())
        for j in range(1, n_row):
            row_copy(chunk, lax.rem(row + j, n_row)).wait_send()
        return carry

    lax.fori_loop(0, CHUNKS, drain, 0)

    @pl.when(has_previous)
    def _():
        pass_state.wait_send()
        pass_rim.wait_send()


def on_device(
    output_grad,
    conv_out,
    input_mix,
    output_mix,
    step_size,
    log_decay,
    skip_gain,
    conv_weight,
    later_grad,
    proj_weight,
):
    n_ctx, n_row, n_col = (lax.axis_size(name) for name in ("ctx", "row", "col"))
    tokens, width = output_grad.shape
    heads = step_size.shape[0]
    states = later_grad.shape[2]
    head_block = lax.axis_index("row") * n_col + lax.axis_index("col")
    group = head_block * heads // HPG
    write_rows = lax.dynamic_index_in_dim(input_mix, group, 1, keepdims=False)
    read_rows = lax.dynamic_index_in_dim(output_mix, group, 1, keepdims=False)
    step = tokens // CHUNKS
    d_out = proj_weight.shape[0] // n_row
    in_vmem = pl.BlockSpec(memory_space=pltpu.VMEM)
    bf16, f32 = jnp.bfloat16, jnp.float32
    hidden_grad, x_grad, state_grad = pl.pallas_call(
        functools.partial(layer_kernel, n_ctx, n_row, n_col),
        out_shape=(
            jax.ShapeDtypeStruct((tokens, d_out), bf16),
            jax.ShapeDtypeStruct((tokens, width), bf16),
            jax.ShapeDtypeStruct((width, states), f32),
        ),
        in_specs=[in_vmem] * 9 + [pl.BlockSpec(memory_space=pl.ANY)],
        out_specs=(in_vmem,) * 3,
        scratch_shapes=[
            pltpu.VMEM(proj_weight.shape, bf16),
            pltpu.VMEM((tokens + RIM, width), f32),
            pltpu.VMEM((width, states), f32),
            pltpu.VMEM((width, states), bf16),
            pltpu.VMEM((width, states), bf16),
            pltpu.VMEM((RIM, width), bf16),
            pltpu.VMEM((RIM, width), bf16),
            pltpu.VMEM((CHUNKS, n_col, step, width), bf16),
            pltpu.VMEM((CHUNKS, n_row, step, d_out), bf16),
            pltpu.VMEM((CHUNKS, n_row, step, d_out), bf16),
            pltpu.VMEM((CHUNKS, step, d_out), f32),
            pltpu.SemaphoreType.DMA,
            pltpu.SemaphoreType.DMA((CHUNKS, 2 * REACH)),
            pltpu.SemaphoreType.DMA((CHUNKS, n_col)),
            pltpu.SemaphoreType.DMA((CHUNKS, 2, n_col)),
            pltpu.SemaphoreType.DMA((CHUNKS, n_row)),
            pltpu.SemaphoreType.DMA((CHUNKS, n_row)),
            pltpu.SemaphoreType.DMA((2,)),
            pltpu.SemaphoreType.DMA((2,)),
        ],
        compiler_params=pltpu.CompilerParams(
            collective_id=0, has_side_effects=True, vmem_limit_bytes=48 << 20
        ),
    )(
        output_grad,
        conv_out,
        write_rows,
        read_rows,
        step_size,
        log_decay,
        jnp.repeat(skip_gain, HD)[None, :],
        conv_weight,
        later_grad.reshape(width, states),
        proj_weight,
    )
    return (hidden_grad, x_grad, state_grad.reshape(1, heads, HD, states))


def solution(mesh):
    return jax.shard_map(
        on_device,
        mesh=mesh,
        in_specs=(
            P("ctx", ("row", "col")),
            P("ctx", ("row", "col")),
            P("ctx", None, None),
            P("ctx", None, None),
            P(("row", "col"), "ctx"),
            P(("row", "col"), "ctx"),
            P(("row", "col")),
            P(None, ("row", "col")),
            P(("row", "col"), None, None),
            P("col", "row"),
        ),
        out_specs=(
            P("ctx", ("col", "row")),
            P("ctx", ("row", "col")),
            P("ctx", ("row", "col"), None, None),
        ),
        check_vma=False,
    )
```

```python
import functools

import jax
import jax.numpy as jnp
from jax import lax
from jax.experimental import pallas as pl
from jax.experimental.pallas import tpu as pltpu
from jax.sharding import PartitionSpec as P

HD = 64
HPG = 32
KW = 4
PARTS = (3, 4, 4, 3, 2)
REACH = 2
FLYING = 3
RIM = 16
VMEM_MIB = 60


def layer_kernel(
    n_ctx,
    n_row,
    n_col,
    grad_hbm,
    conv_hbm,
    step_hbm,
    decay_hbm,
    skip_hbm,
    tap_hbm,
    later_hbm,
    w_hbm,
    write_ref,
    read_ref,
    out_hbm,
    x_hbm,
    state_hbm,
    out_ref,
    state_ref,
    grad_ref,
    conv_ref,
    step_ref,
    decay_ref,
    skip_ref,
    tap_ref,
    w_ref,
    pre_ref,
    carried_ref,
    state_out,
    state_in,
    rim_out,
    rim_in,
    gathered,
    staged,
    landed,
    own,
    load_sem,
    store_sem,
    col_send,
    col_recv,
    fwd_send,
    row_send,
    row_recv,
    ctx_send,
    ctx_recv,
):
    ctx = lax.axis_index("ctx")
    row = lax.axis_index("row")
    col = lax.axis_index("col")
    tokens, width = grad_ref.shape
    d_out = out_ref.shape[1]
    mesh_id = pl.DeviceIdType.MESH
    has_next, has_previous = ctx < n_ctx - 1, ctx > 0

    sizes = [tokens // sum(PARTS) * part for part in PARTS]
    starts = [tokens - sum(sizes[: at + 1]) for at in range(len(PARTS))]
    spans = [pl.ds(start, size) for start, size in zip(starts, sizes)]
    chunks = range(len(PARTS))

    pairs_of_refs = (
        (decay_hbm, decay_ref),
        (grad_hbm, grad_ref),
        (step_hbm, step_ref),
        (skip_hbm, skip_ref),
        (tap_hbm, tap_ref),
        (conv_hbm, conv_ref),
        (w_hbm, w_ref),
    )
    loads = [
        pltpu.make_async_copy(source, target, load_sem.at[at])
        for at, (source, target) in enumerate(pairs_of_refs)
    ]
    load_decay, load_grad, load_step, load_skip, load_tap, load_conv, load_w = loads
    load_later = pltpu.make_async_copy(later_hbm, carried_ref, load_sem.at[len(loads)])
    for load in loads[:-1]:
        load.start()
    store_out = [
        pltpu.make_async_copy(out_ref.at[span], out_hbm.at[span], store_sem.at[0, at])
        for at, span in enumerate(spans)
    ]
    store_x = [
        pltpu.make_async_copy(gathered.at[col, span], x_hbm.at[span], store_sem.at[1, at])
        for at, span in enumerate(spans)
    ]
    store_state = pltpu.make_async_copy(state_ref, state_hbm, store_sem.at[2, 0])

    @pl.when(jnp.logical_not(has_next))
    def _():
        load_later.start()

    load_w.start()

    barrier = pltpu.get_barrier_semaphore()
    for j in range(1, n_row):
        pl.semaphore_signal(
            barrier, inc=1, device_id={"row": lax.rem(row + j, n_row)}, device_id_type=mesh_id
        )
    for j in range(1, n_col):
        pl.semaphore_signal(
            barrier, inc=1, device_id={"col": lax.rem(col + j, n_col)}, device_id_type=mesh_id
        )
    for there, delta in ((has_next, 1), (has_previous, -1)):

        @pl.when(there)
        def _():
            pl.semaphore_signal(
                barrier, inc=1, device_id={"ctx": ctx + delta}, device_id_type=mesh_id
            )

    deltas = [d for d in range(-REACH, REACH + 1) if d != 0]

    def col_copy(chunk, owner, target, sem):
        return pltpu.make_async_remote_copy(
            src_ref=gathered.at[owner, spans[chunk]],
            dst_ref=gathered.at[owner, spans[chunk]],
            send_sem=sem,
            recv_sem=col_recv.at[chunk, owner],
            device_id={"col": target},
            device_id_type=mesh_id,
        )

    def each_send(chunk, act):
        for at, delta in enumerate(deltas):
            target = col + delta

            @pl.when((target >= 0) & (target < n_col))
            def _():
                act(col_copy(chunk, col, target, col_send.at[chunk, at]))

    def send_chunk(chunk):
        each_send(chunk, lambda copy: copy.start())

    def each_arrival(chunk, receive, forward):
        for side, sign in enumerate((-1, 1)):
            for dist in list(range(REACH, n_col)) + list(range(1, REACH)):
                owner = col + sign * dist

                @pl.when((owner >= 0) & (owner < n_col))
                def _():
                    if receive:
                        col_copy(chunk, owner, col, fwd_send.at[chunk, side, dist]).wait_recv()
                    if dist >= REACH:
                        target = col - sign

                        @pl.when((target >= 0) & (target < n_col))
                        def _():
                            forward(
                                col_copy(chunk, owner, target, fwd_send.at[chunk, side, dist])
                            )

    def row_copy(chunk, target):
        return pltpu.make_async_remote_copy(
            src_ref=staged.at[target, spans[chunk]],
            dst_ref=landed.at[row, spans[chunk]],
            send_sem=row_send.at[chunk, target],
            recv_sem=row_recv.at[chunk, row],
            device_id={"row": target},
            device_id_type=mesh_id,
        )

    def finish(chunk):
        total = own[spans[chunk]]
        for j in range(1, n_row):
            source = lax.rem(row + j, n_row)
            pltpu.make_async_remote_copy(
                src_ref=staged.at[source, spans[chunk]],
                dst_ref=landed.at[source, spans[chunk]],
                send_sem=row_send.at[chunk, source],
                recv_sem=row_recv.at[chunk, source],
                device_id={"row": source},
                device_id_type=mesh_id,
            ).wait_recv()
            total = total + landed[source, spans[chunk]].astype(jnp.float32)
        out_ref[spans[chunk], :] = total.astype(out_ref.dtype)
        store_out[chunk].start()

    def product(chunk, target):
        rows = pl.ds(pl.multiple_of(target * d_out, d_out), d_out)
        total = None
        for owner in range(n_col):
            part = lax.dot_general(
                gathered[owner, spans[chunk]],
                w_ref[rows, owner * width : (owner + 1) * width],
                (((1,), (1,)), ((), ())),
                preferred_element_type=jnp.float32,
            )
            total = part if total is None else total + part
        return total

    def ctx_copy(at, source, target):
        return pltpu.make_async_remote_copy(
            src_ref=source,
            dst_ref=target,
            send_sem=ctx_send.at[at],
            recv_sem=ctx_recv.at[at],
            device_id={"ctx": lax.rem(ctx + n_ctx - 1, n_ctx)},
            device_id_type=mesh_id,
        )

    pass_state = ctx_copy(0, state_out, state_in)
    pass_rim = ctx_copy(1, rim_out, rim_in)

    heads = decay_ref.shape[0]
    pairs = heads // 2
    lanes = 2 * HD
    f32, bf16 = jnp.float32, jnp.bfloat16

    def dot(a, b, a_dim, b_dim):
        return lax.dot_general(
            a, b, (((a_dim,), (b_dim,)), ((), ())), preferred_element_type=f32
        )

    load_decay.wait()
    decay = decay_ref[...]
    high = decay.astype(bf16)
    rest = decay - high.astype(f32)
    middle = rest.astype(bf16)
    low = (rest - middle.astype(f32)).astype(bf16)
    upto = lax.broadcasted_iota(jnp.int32, (tokens, tokens), 0) <= lax.broadcasted_iota(
        jnp.int32, (tokens, tokens), 1
    )
    triangle = upto.astype(f32).astype(bf16)
    cumulative = (
        dot(high, triangle, 1, 0) + dot(middle, triangle, 1, 0) + dot(low, triangle, 1, 0)
    )
    by_token = cumulative.T
    grown = jnp.exp(by_token)
    left = jnp.exp(by_token[tokens - 1 : tokens, :] - by_token)

    def spread(columns, pair, count):
        lane = lax.broadcasted_iota(jnp.int32, (count, lanes), 1)
        return jnp.where(
            lane < HD, columns[:, 2 * pair : 2 * pair + 1], columns[:, 2 * pair + 1 : 2 * pair + 2]
        )

    load_grad.wait()
    weighted = jnp.concatenate(
        [
            (
                spread(grown, pair, tokens)
                * grad_ref[:, pair * lanes : (pair + 1) * lanes].astype(f32)
            ).astype(bf16)
            for pair in range(pairs)
        ],
        axis=1,
    )
    block_sum = dot(weighted, read_ref[...], 0, 0)

    total_signals = n_row + n_col - 2 + has_next.astype(jnp.int32) + has_previous.astype(jnp.int32)
    pl.semaphore_wait(barrier, total_signals)

    @pl.when(has_next)
    def _():
        pass_state.wait_recv()
        carried_ref[...] = state_in[...].astype(f32)

    @pl.when(jnp.logical_not(has_next))
    def _():
        load_later.wait()

    for head in range(heads):
        rows = slice(head * HD, (head + 1) * HD)
        factor = jnp.exp(cumulative[head : head + 1, tokens - 1 : tokens])
        state = block_sum[rows] + factor * carried_ref[rows, :]
        state_ref[rows, :] = state
        state_out[rows, :] = state.astype(bf16)

    @pl.when(has_previous)
    def _():
        pass_state.start()

    store_state.start()
    carried = carried_ref[...].astype(bf16)
    for load in (load_step, load_skip, load_tap, load_conv):
        load.wait()
    steps = step_ref[...].T
    skips = skip_ref[...]

    def pre_rows(start, count):
        rows = slice(start, start + count)
        span = tokens - start
        write = write_ref[rows, :]
        scores = dot(write, read_ref[start:, :], 1, 1)
        later = lax.broadcasted_iota(jnp.int32, (count, span), 1) >= lax.broadcasted_iota(
            jnp.int32, (count, span), 0
        )
        scores = jnp.where(later, scores, 0.0)
        inter = dot(write, carried, 1, 1)
        lane = lax.broadcasted_iota(jnp.int32, (count, lanes), 1)
        found = []
        for pair in range(pairs):
            columns = slice(pair * lanes, (pair + 1) * lanes)
            mixing = []
            for head in (2 * pair, 2 * pair + 1):
                offset = cumulative[head : head + 1, start:] - by_token[rows, head : head + 1]
                mixing.append((jnp.exp(jnp.minimum(offset, 0.0)) * scores).astype(bf16))
            both = dot(jnp.concatenate(mixing, axis=0), grad_ref[start:, columns], 1, 0)
            intra = jnp.where(lane < HD, both[:count], both[count:])
            summed = intra + inter[:, columns] * spread(left[rows], pair, count)
            value = (
                spread(steps[rows], pair, count) * summed
                + spread(skips, pair, 1) * grad_ref[rows, columns].astype(f32)
            )
            v = conv_ref[rows, columns].astype(f32)
            q = 1.0 / (1.0 + jnp.exp(-v))
            found.append((value * q * (1.0 + v * (1.0 - q))).astype(bf16))
        return jnp.concatenate(found, axis=1)

    @pl.when(has_previous)
    def _():
        rim_out[...] = pre_rows(0, RIM)
        pass_rim.start()

    for chunk in chunks:
        start, step = starts[chunk], sizes[chunk]
        pre_ref[start : start + step, :] = pre_rows(start, step).astype(f32)
        if chunk == 0:

            @pl.when(has_next)
            def _():
                pass_rim.wait_recv()
                pre_ref[tokens:, :] = rim_in[...].astype(f32)

            @pl.when(jnp.logical_not(has_next))
            def _():
                pre_ref[tokens:, :] = jnp.zeros((RIM, pre_ref.shape[1]), f32)

        mixed = tap_ref[0:1, :] * pre_ref[start : start + step, :]
        for tap in range(1, KW):
            mixed = mixed + tap_ref[tap : tap + 1, :] * pre_ref[start + tap : start + tap + step, :]
        mixed = mixed.astype(bf16)
        gathered[col, spans[chunk]] = mixed
        store_x[chunk].start()
        if chunk < FLYING:
            send_chunk(chunk)
    load_w.wait()

    for chunk in chunks:
        each_arrival(chunk, True, lambda copy: copy.start())
        each_send(chunk, lambda copy: copy.wait_send())
        if chunk + FLYING < len(PARTS):
            send_chunk(chunk + FLYING)

        @pl.loop(1, n_row)
        def _(j):
            target = lax.rem(row + j, n_row)
            staged[target, spans[chunk]] = product(chunk, target).astype(bf16)
            row_copy(chunk, target).start()

        own[spans[chunk]] = product(chunk, row)
        if chunk > 0:
            finish(chunk - 1)

    finish(len(PARTS) - 1)
    for chunk in chunks:
        each_arrival(chunk, False, lambda copy: copy.wait_send())
        for j in range(1, n_row):
            row_copy(chunk, lax.rem(row + j, n_row)).wait_send()

    @pl.when(has_previous)
    def _():
        pass_state.wait_send()
        pass_rim.wait_send()

    for store in (*store_out, *store_x, store_state):
        store.wait()


def hand_over(*refs):
    sems = refs[6]
    copies = [pltpu.make_async_copy(refs[at], refs[3 + at], sems.at[at]) for at in range(3)]
    for copy in copies:
        copy.start()
    for copy in copies:
        copy.wait()


def on_device(
    output_grad,
    conv_out,
    input_mix,
    output_mix,
    step_size,
    log_decay,
    skip_gain,
    conv_weight,
    later_grad,
    proj_weight,
):
    n_ctx, n_row, n_col = (lax.axis_size(name) for name in ("ctx", "row", "col"))
    tokens, width = output_grad.shape
    heads = step_size.shape[0]
    states = later_grad.shape[2]
    head_block = lax.axis_index("row") * n_col + lax.axis_index("col")
    group = head_block * heads // HPG
    write_rows = lax.dynamic_index_in_dim(input_mix, group, 1, keepdims=False)
    read_rows = lax.dynamic_index_in_dim(output_mix, group, 1, keepdims=False)
    d_out = proj_weight.shape[0] // n_row
    in_vmem = pl.BlockSpec(memory_space=pltpu.VMEM)
    anywhere = pl.BlockSpec(memory_space=pl.ANY)
    bf16, f32 = jnp.bfloat16, jnp.float32
    outputs = (
        jax.ShapeDtypeStruct((tokens, d_out), bf16),
        jax.ShapeDtypeStruct((tokens, width), bf16),
        jax.ShapeDtypeStruct((width, states), f32),
    )
    loaded = (
        output_grad,
        conv_out,
        step_size,
        log_decay,
        skip_gain.reshape(1, heads),
        conv_weight,
        later_grad.reshape(width, states),
        proj_weight,
    )
    results = pl.pallas_call(
        functools.partial(layer_kernel, n_ctx, n_row, n_col),
        out_shape=outputs,
        in_specs=[pl.BlockSpec(memory_space=pltpu.HBM)] * len(loaded) + [in_vmem] * 2,
        out_specs=(anywhere,) * 3,
        scratch_shapes=[
            pltpu.VMEM((tokens, d_out), bf16),
            pltpu.VMEM((width, states), f32),
            *(pltpu.VMEM(array.shape, array.dtype) for array in loaded[:6]),
            pltpu.VMEM(proj_weight.shape, bf16),
            pltpu.VMEM((tokens + RIM, width), f32),
            pltpu.VMEM((width, states), f32),
            pltpu.VMEM((width, states), bf16),
            pltpu.VMEM((width, states), bf16),
            pltpu.VMEM((RIM, width), bf16),
            pltpu.VMEM((RIM, width), bf16),
            pltpu.VMEM((n_col, tokens, width), bf16),
            pltpu.VMEM((n_row, tokens, d_out), bf16),
            pltpu.VMEM((n_row, tokens, d_out), bf16),
            pltpu.VMEM((tokens, d_out), f32),
            pltpu.SemaphoreType.DMA((len(loaded),)),
            pltpu.SemaphoreType.DMA((3, len(PARTS))),
            pltpu.SemaphoreType.DMA((len(PARTS), 2 * REACH)),
            pltpu.SemaphoreType.DMA((len(PARTS), n_col)),
            pltpu.SemaphoreType.DMA((len(PARTS), 2, n_col)),
            pltpu.SemaphoreType.DMA((len(PARTS), n_row)),
            pltpu.SemaphoreType.DMA((len(PARTS), n_row)),
            pltpu.SemaphoreType.DMA((2,)),
            pltpu.SemaphoreType.DMA((2,)),
        ],
        compiler_params=pltpu.CompilerParams(
            collective_id=0, has_side_effects=True, vmem_limit_bytes=VMEM_MIB << 20
        ),
    )(*loaded, write_rows, read_rows)
    hidden_grad, x_grad, state_grad = pl.pallas_call(
        hand_over,
        out_shape=outputs,
        in_specs=[anywhere] * 3,
        out_specs=(anywhere,) * 3,
        scratch_shapes=[pltpu.SemaphoreType.DMA((3,))],
        compiler_params=pltpu.CompilerParams(vmem_limit_bytes=VMEM_MIB << 20),
    )(*results)
    return (hidden_grad, x_grad, state_grad.reshape(1, heads, HD, states))


def solution(mesh):
    return jax.shard_map(
        on_device,
        mesh=mesh,
        in_specs=(
            P("ctx", ("row", "col")),
            P("ctx", ("row", "col")),
            P("ctx", None, None),
            P("ctx", None, None),
            P(("row", "col"), "ctx"),
            P(("row", "col"), "ctx"),
            P(("row", "col")),
            P(None, ("row", "col")),
            P(("row", "col"), None, None),
            P("col", "row"),
        ),
        out_specs=(
            P("ctx", ("col", "row")),
            P("ctx", ("row", "col")),
            P("ctx", ("row", "col"), None, None),
        ),
        check_vma=False,
    )
```

```python
import functools

import jax
import jax.numpy as jnp
from jax import lax
from jax.experimental import pallas as pl
from jax.experimental.pallas import tpu as pltpu
from jax.sharding import PartitionSpec as P

HD = 64
HPG = 32
KW = 4
PARTS = (4, 4, 3, 3, 2)
REACH = 2
FLYING = 2
RIM = 16
VMEM_MIB = 60


def layer_kernel(
    n_ctx,
    n_row,
    n_col,
    grad_hbm,
    conv_hbm,
    step_hbm,
    decay_hbm,
    skip_hbm,
    tap_hbm,
    later_hbm,
    w_hbm,
    write_ref,
    read_ref,
    out_hbm,
    x_hbm,
    state_hbm,
    out_ref,
    state_ref,
    grad_ref,
    conv_ref,
    step_ref,
    decay_ref,
    skip_ref,
    tap_ref,
    w_ref,
    pre_ref,
    carried_ref,
    state_out,
    state_in,
    rim_out,
    rim_in,
    gathered,
    staged,
    landed,
    own,
    load_sem,
    store_sem,
    col_send,
    col_recv,
    fwd_send,
    row_send,
    row_recv,
    ctx_send,
    ctx_recv,
):
    ctx = lax.axis_index("ctx")
    row = lax.axis_index("row")
    col = lax.axis_index("col")
    tokens, width = grad_ref.shape
    d_out = out_ref.shape[1]
    mesh_id = pl.DeviceIdType.MESH
    has_next, has_previous = ctx < n_ctx - 1, ctx > 0

    sizes = [tokens // sum(PARTS) * part for part in PARTS]
    starts = [tokens - sum(sizes[: at + 1]) for at in range(len(PARTS))]
    spans = [pl.ds(start, size) for start, size in zip(starts, sizes)]
    chunks = range(len(PARTS))

    pairs_of_refs = (
        (decay_hbm, decay_ref),
        (grad_hbm, grad_ref),
        (step_hbm, step_ref),
        (skip_hbm, skip_ref),
        (tap_hbm, tap_ref),
        (conv_hbm, conv_ref),
        (w_hbm, w_ref),
    )
    loads = [
        pltpu.make_async_copy(source, target, load_sem.at[at])
        for at, (source, target) in enumerate(pairs_of_refs)
    ]
    load_decay, load_grad, load_step, load_skip, load_tap, load_conv, load_w = loads
    load_later = pltpu.make_async_copy(later_hbm, carried_ref, load_sem.at[len(loads)])
    for load in loads[:-1]:
        load.start()
    store_out = [
        pltpu.make_async_copy(out_ref.at[span], out_hbm.at[span], store_sem.at[0, at])
        for at, span in enumerate(spans)
    ]
    store_x = [
        pltpu.make_async_copy(gathered.at[col, span], x_hbm.at[span], store_sem.at[1, at])
        for at, span in enumerate(spans)
    ]
    store_state = pltpu.make_async_copy(state_ref, state_hbm, store_sem.at[2, 0])

    @pl.when(jnp.logical_not(has_next))
    def _():
        load_later.start()

    load_w.start()

    barrier = pltpu.get_barrier_semaphore()
    for j in range(1, n_row):
        pl.semaphore_signal(
            barrier, inc=1, device_id={"row": lax.rem(row + j, n_row)}, device_id_type=mesh_id
        )
    for j in range(1, n_col):
        pl.semaphore_signal(
            barrier, inc=1, device_id={"col": lax.rem(col + j, n_col)}, device_id_type=mesh_id
        )
    for there, delta in ((has_next, 1), (has_previous, -1)):

        @pl.when(there)
        def _():
            pl.semaphore_signal(
                barrier, inc=1, device_id={"ctx": ctx + delta}, device_id_type=mesh_id
            )

    deltas = [d for d in range(-REACH, REACH + 1) if d != 0]

    def col_copy(chunk, owner, target, sem):
        return pltpu.make_async_remote_copy(
            src_ref=gathered.at[owner, spans[chunk]],
            dst_ref=gathered.at[owner, spans[chunk]],
            send_sem=sem,
            recv_sem=col_recv.at[chunk, owner],
            device_id={"col": target},
            device_id_type=mesh_id,
        )

    def each_send(chunk, act):
        for at, delta in enumerate(deltas):
            target = col + delta

            @pl.when((target >= 0) & (target < n_col))
            def _():
                act(col_copy(chunk, col, target, col_send.at[chunk, at]))

    def send_chunk(chunk):
        each_send(chunk, lambda copy: copy.start())

    def each_arrival(chunk, receive, forward):
        for side, sign in enumerate((-1, 1)):
            for dist in list(range(REACH, n_col)) + list(range(1, REACH)):
                owner = col + sign * dist

                @pl.when((owner >= 0) & (owner < n_col))
                def _():
                    if receive:
                        col_copy(chunk, owner, col, fwd_send.at[chunk, side, dist]).wait_recv()
                    if dist >= REACH:
                        target = col - sign

                        @pl.when((target >= 0) & (target < n_col))
                        def _():
                            forward(
                                col_copy(chunk, owner, target, fwd_send.at[chunk, side, dist])
                            )

    def row_copy(chunk, target):
        return pltpu.make_async_remote_copy(
            src_ref=staged.at[target, spans[chunk]],
            dst_ref=landed.at[row, spans[chunk]],
            send_sem=row_send.at[chunk, target],
            recv_sem=row_recv.at[chunk, row],
            device_id={"row": target},
            device_id_type=mesh_id,
        )

    def finish(chunk):
        total = own[spans[chunk]]
        for j in range(1, n_row):
            source = lax.rem(row + j, n_row)
            pltpu.make_async_remote_copy(
                src_ref=staged.at[source, spans[chunk]],
                dst_ref=landed.at[source, spans[chunk]],
                send_sem=row_send.at[chunk, source],
                recv_sem=row_recv.at[chunk, source],
                device_id={"row": source},
                device_id_type=mesh_id,
            ).wait_recv()
            total = total + landed[source, spans[chunk]].astype(jnp.float32)
        out_ref[spans[chunk], :] = total.astype(out_ref.dtype)
        store_out[chunk].start()

    def product(chunk, target):
        rows = pl.ds(pl.multiple_of(target * d_out, d_out), d_out)
        total = None
        for owner in range(n_col):
            part = lax.dot_general(
                gathered[owner, spans[chunk]],
                w_ref[rows, owner * width : (owner + 1) * width],
                (((1,), (1,)), ((), ())),
                preferred_element_type=jnp.float32,
            )
            total = part if total is None else total + part
        return total

    def ctx_copy(at, source, target):
        return pltpu.make_async_remote_copy(
            src_ref=source,
            dst_ref=target,
            send_sem=ctx_send.at[at],
            recv_sem=ctx_recv.at[at],
            device_id={"ctx": lax.rem(ctx + n_ctx - 1, n_ctx)},
            device_id_type=mesh_id,
        )

    pass_state = ctx_copy(0, state_out, state_in)
    pass_rim = ctx_copy(1, rim_out, rim_in)

    heads = decay_ref.shape[0]
    pairs = heads // 2
    lanes = 2 * HD
    f32, bf16 = jnp.float32, jnp.bfloat16

    def dot(a, b, a_dim, b_dim):
        return lax.dot_general(
            a, b, (((a_dim,), (b_dim,)), ((), ())), preferred_element_type=f32
        )

    load_decay.wait()
    decay = decay_ref[...]
    high = decay.astype(bf16)
    rest = decay - high.astype(f32)
    middle = rest.astype(bf16)
    low = (rest - middle.astype(f32)).astype(bf16)
    upto = lax.broadcasted_iota(jnp.int32, (tokens, tokens), 0) <= lax.broadcasted_iota(
        jnp.int32, (tokens, tokens), 1
    )
    triangle = upto.astype(f32).astype(bf16)
    cumulative = (
        dot(high, triangle, 1, 0) + dot(middle, triangle, 1, 0) + dot(low, triangle, 1, 0)
    )
    by_token = cumulative.T
    grown = jnp.exp(by_token)
    left = jnp.exp(by_token[tokens - 1 : tokens, :] - by_token)

    def spread(columns, pair, count):
        lane = lax.broadcasted_iota(jnp.int32, (count, lanes), 1)
        return jnp.where(
            lane < HD, columns[:, 2 * pair : 2 * pair + 1], columns[:, 2 * pair + 1 : 2 * pair + 2]
        )

    load_grad.wait()
    weighted = jnp.concatenate(
        [
            (
                spread(grown, pair, tokens)
                * grad_ref[:, pair * lanes : (pair + 1) * lanes].astype(f32)
            ).astype(bf16)
            for pair in range(pairs)
        ],
        axis=1,
    )
    block_sum = dot(weighted, read_ref[...], 0, 0)

    total_signals = n_row + n_col - 2 + has_next.astype(jnp.int32) + has_previous.astype(jnp.int32)
    pl.semaphore_wait(barrier, total_signals)

    @pl.when(has_next)
    def _():
        pass_state.wait_recv()
        carried_ref[...] = state_in[...].astype(f32)

    @pl.when(jnp.logical_not(has_next))
    def _():
        load_later.wait()

    for head in range(heads):
        rows = slice(head * HD, (head + 1) * HD)
        factor = jnp.exp(cumulative[head : head + 1, tokens - 1 : tokens])
        state = block_sum[rows] + factor * carried_ref[rows, :]
        state_ref[rows, :] = state
        state_out[rows, :] = state.astype(bf16)

    @pl.when(has_previous)
    def _():
        pass_state.start()

    store_state.start()
    carried = carried_ref[...].astype(bf16)
    for load in (load_step, load_skip, load_tap, load_conv):
        load.wait()
    steps = step_ref[...].T
    skips = skip_ref[...]

    def pre_rows(start, count):
        rows = slice(start, start + count)
        span = tokens - start
        write = write_ref[rows, :]
        scores = dot(write, read_ref[start:, :], 1, 1)
        later = lax.broadcasted_iota(jnp.int32, (count, span), 1) >= lax.broadcasted_iota(
            jnp.int32, (count, span), 0
        )
        scores = jnp.where(later, scores, 0.0)
        inter = dot(write, carried, 1, 1)
        lane = lax.broadcasted_iota(jnp.int32, (count, lanes), 1)
        found = []
        for pair in range(pairs):
            columns = slice(pair * lanes, (pair + 1) * lanes)
            mixing = []
            for head in (2 * pair, 2 * pair + 1):
                offset = cumulative[head : head + 1, start:] - by_token[rows, head : head + 1]
                mixing.append((jnp.exp(jnp.minimum(offset, 0.0)) * scores).astype(bf16))
            both = dot(jnp.concatenate(mixing, axis=0), grad_ref[start:, columns], 1, 0)
            intra = jnp.where(lane < HD, both[:count], both[count:])
            summed = intra + inter[:, columns] * spread(left[rows], pair, count)
            value = (
                spread(steps[rows], pair, count) * summed
                + spread(skips, pair, 1) * grad_ref[rows, columns].astype(f32)
            )
            v = conv_ref[rows, columns].astype(f32)
            q = 1.0 / (1.0 + jnp.exp(-v))
            found.append((value * q * (1.0 + v * (1.0 - q))).astype(bf16))
        return jnp.concatenate(found, axis=1)

    @pl.when(has_previous)
    def _():
        rim_out[...] = pre_rows(0, RIM)
        pass_rim.start()

    for chunk in chunks:
        start, step = starts[chunk], sizes[chunk]
        pre_ref[start : start + step, :] = pre_rows(start, step).astype(f32)
        if chunk == 0:

            @pl.when(has_next)
            def _():
                pass_rim.wait_recv()
                pre_ref[tokens:, :] = rim_in[...].astype(f32)

            @pl.when(jnp.logical_not(has_next))
            def _():
                pre_ref[tokens:, :] = jnp.zeros((RIM, pre_ref.shape[1]), f32)

        mixed = tap_ref[0:1, :] * pre_ref[start : start + step, :]
        for tap in range(1, KW):
            mixed = mixed + tap_ref[tap : tap + 1, :] * pre_ref[start + tap : start + tap + step, :]
        mixed = mixed.astype(bf16)
        gathered[col, spans[chunk]] = mixed
        store_x[chunk].start()
        if chunk < FLYING:
            send_chunk(chunk)
    load_w.wait()

    for chunk in chunks:
        each_arrival(chunk, True, lambda copy: copy.start())
        each_send(chunk, lambda copy: copy.wait_send())
        if chunk + FLYING < len(PARTS):
            send_chunk(chunk + FLYING)

        @pl.loop(1, n_row)
        def _(j):
            target = lax.rem(row + j, n_row)
            staged[target, spans[chunk]] = product(chunk, target).astype(bf16)
            row_copy(chunk, target).start()

        own[spans[chunk]] = product(chunk, row)
        if chunk > 0:
            finish(chunk - 1)

    finish(len(PARTS) - 1)
    for chunk in chunks:
        each_arrival(chunk, False, lambda copy: copy.wait_send())
        for j in range(1, n_row):
            row_copy(chunk, lax.rem(row + j, n_row)).wait_send()

    @pl.when(has_previous)
    def _():
        pass_state.wait_send()
        pass_rim.wait_send()

    for store in (*store_out, *store_x, store_state):
        store.wait()


def hand_over(*refs):
    count = len(refs) // 3
    sources, targets, kept, sems = refs[:count], refs[count : 2 * count], refs[2 * count : -1], refs[-1]
    takes = [pltpu.make_async_copy(sources[at], kept[at], sems.at[0, at]) for at in range(count)]
    gives = [pltpu.make_async_copy(kept[at], targets[at], sems.at[1, at]) for at in range(count)]
    for take in takes:
        take.start()
    for take, give in zip(takes, gives):
        take.wait()
        give.start()
    for give in gives:
        give.wait()


def on_device(
    output_grad,
    conv_out,
    input_mix,
    output_mix,
    step_size,
    log_decay,
    skip_gain,
    conv_weight,
    later_grad,
    proj_weight,
):
    n_ctx, n_row, n_col = (lax.axis_size(name) for name in ("ctx", "row", "col"))
    tokens, width = output_grad.shape
    heads = step_size.shape[0]
    states = later_grad.shape[2]
    head_block = lax.axis_index("row") * n_col + lax.axis_index("col")
    group = head_block * heads // HPG
    write_rows = lax.dynamic_index_in_dim(input_mix, group, 1, keepdims=False)
    read_rows = lax.dynamic_index_in_dim(output_mix, group, 1, keepdims=False)
    d_out = proj_weight.shape[0] // n_row
    in_vmem = pl.BlockSpec(memory_space=pltpu.VMEM)
    anywhere = pl.BlockSpec(memory_space=pl.ANY)
    bf16, f32 = jnp.bfloat16, jnp.float32
    outputs = (
        jax.ShapeDtypeStruct((tokens, d_out), bf16),
        jax.ShapeDtypeStruct((tokens, width), bf16),
        jax.ShapeDtypeStruct((width, states), f32),
    )
    loaded = (
        output_grad,
        conv_out,
        step_size,
        log_decay,
        skip_gain.reshape(1, heads),
        conv_weight,
        later_grad.reshape(width, states),
        proj_weight,
    )
    results = pl.pallas_call(
        functools.partial(layer_kernel, n_ctx, n_row, n_col),
        out_shape=outputs,
        in_specs=[pl.BlockSpec(memory_space=pltpu.HBM)] * len(loaded) + [in_vmem] * 2,
        out_specs=(anywhere,) * 3,
        scratch_shapes=[
            pltpu.VMEM((tokens, d_out), bf16),
            pltpu.VMEM((width, states), f32),
            *(pltpu.VMEM(array.shape, array.dtype) for array in loaded[:6]),
            pltpu.VMEM(proj_weight.shape, bf16),
            pltpu.VMEM((tokens + RIM, width), f32),
            pltpu.VMEM((width, states), f32),
            pltpu.VMEM((width, states), bf16),
            pltpu.VMEM((width, states), bf16),
            pltpu.VMEM((RIM, width), bf16),
            pltpu.VMEM((RIM, width), bf16),
            pltpu.VMEM((n_col, tokens, width), bf16),
            pltpu.VMEM((n_row, tokens, d_out), bf16),
            pltpu.VMEM((n_row, tokens, d_out), bf16),
            pltpu.VMEM((tokens, d_out), f32),
            pltpu.SemaphoreType.DMA((len(loaded),)),
            pltpu.SemaphoreType.DMA((3, len(PARTS))),
            pltpu.SemaphoreType.DMA((len(PARTS), 2 * REACH)),
            pltpu.SemaphoreType.DMA((len(PARTS), n_col)),
            pltpu.SemaphoreType.DMA((len(PARTS), 2, n_col)),
            pltpu.SemaphoreType.DMA((len(PARTS), n_row)),
            pltpu.SemaphoreType.DMA((len(PARTS), n_row)),
            pltpu.SemaphoreType.DMA((2,)),
            pltpu.SemaphoreType.DMA((2,)),
        ],
        compiler_params=pltpu.CompilerParams(
            collective_id=0, has_side_effects=True, vmem_limit_bytes=VMEM_MIB << 20
        ),
    )(*loaded, write_rows, read_rows)
    hidden_grad, x_grad, state_grad = pl.pallas_call(
        hand_over,
        out_shape=outputs,
        in_specs=[anywhere] * 3,
        out_specs=(anywhere,) * 3,
        scratch_shapes=[
            *(pltpu.VMEM(output.shape, output.dtype) for output in outputs),
            pltpu.SemaphoreType.DMA((2, len(outputs))),
        ],
        compiler_params=pltpu.CompilerParams(vmem_limit_bytes=VMEM_MIB << 20),
    )(*results)
    return (hidden_grad, x_grad, state_grad.reshape(1, heads, HD, states))


def solution(mesh):
    return jax.shard_map(
        on_device,
        mesh=mesh,
        in_specs=(
            P("ctx", ("row", "col")),
            P("ctx", ("row", "col")),
            P("ctx", None, None),
            P("ctx", None, None),
            P(("row", "col"), "ctx"),
            P(("row", "col"), "ctx"),
            P(("row", "col")),
            P(None, ("row", "col")),
            P(("row", "col"), None, None),
            P("col", "row"),
        ),
        out_specs=(
            P("ctx", ("col", "row")),
            P("ctx", ("row", "col")),
            P("ctx", ("row", "col"), None, None),
        ),
        check_vma=False,
    )
```
